32 devices in a mesh: dp: 8 (over y, x, core), expert: 4 (over z).
Axes of the slice: x: 2, y: 2, z: 4, core: 2. Of those that a mesh axis runs over, the one named last changes fastest.
Arguments:
- tokens: bfloat16 [8192, 1024], P(('dp', 'expert')), may hold values from -6 to 6
- out_grad: bfloat16 [8192, 1024], P(('dp', 'expert')), may hold values from -6 to 6
- gate: float32 [8192], P(('dp', 'expert')), may hold values from 0.2 to 1
- region: int32 [8192, 1], P(('dp', 'expert')), may hold values from 0 to 3; in each aligned block of 256 rows (0 to 255, 256 to 511, ...) at most 128 rows name the same one
- w_in: bfloat16 [4, 4096, 1024], P('expert'), may hold values from -0.1875 to 0.1875
- w_out: bfloat16 [4, 4096, 1024], P('expert'), may hold values from -0.09375 to 0.09375
Outputs:
- token_grad: bfloat16 [8192, 1024], P(('dp', 'expert'))
- w_in_grad: float32 [4, 4096, 1024], P('expert', 'dp')
- w_out_grad: float32 [4, 4096, 1024], P('expert', 'dp')
The draws below stay inside these ranges and needn't reach their ends.
Inputs may be any that keep to these rules, and one draw needn't show every extreme that they name: `region`: of the 256 rows of one device, at most 128 name the same expert, and in every draw some device has exactly 128 rows for some expert.
All inputs are finite; a program needn't handle non-finite values.
Results may differ from the reference program's by a relative error of at most 0.02.
Values may be sent and summed in bfloat16 or wider, within the bound.
A program may use at most 128 MiB of HBM per device.

```python
import math
import jax
import jax.numpy as jnp
import numpy as np
from jax import lax

D = 1024
FF = 4096
TOK_DEV = 256
EXPERTS = 4
CAP = 128
TOKENS = 8192
N_DP = 8
N_EXPERT = 4


def level_of(key, shape, cuts, smallest, high):
    loudness, own = 1.0, jax.random.fold_in(key, 6)
    for axis_at, shards_of in cuts:
        draws = jnp.exp(jax.random.uniform(jax.random.fold_in(own, axis_at), (shards_of,), jnp.float32, smallest / len(cuts), high / len(cuts)))
        loudness = loudness * jnp.repeat(draws, shape[axis_at] // shards_of).reshape([-1 if axis == axis_at else 1 for axis in range(len(shape))])
    return loudness


def routed_block(rng, own, number, rows, amount, top, reach, slope):
    order = jax.random.permutation(rng, amount)
    heavy_load, usual = shares(amount, rows * top, reach, slope, True), shares(amount, rows * top, reach, slope, False)
    places = jnp.arange(amount)

    def named(tallies, offset_by):
        used = int((tallies > 0).sum())
        fixed = max(1, used // 4)
        passed = fixed + (places - fixed + offset_by * (used - fixed)) % max(1, amount - fixed)
        return jnp.zeros((amount,), jnp.int32).at[order[jnp.where(places < fixed, places, passed)]].set(jnp.asarray(tallies, jnp.int32))

    tallies = jnp.where(number % 4 == 0, named(heavy_load, number // 4), named(usual, number - number // 4 - 1))
    mixed = jax.random.permutation(jax.random.fold_in(own, 3), amount)
    giver, sink = mixed[0:amount // 2 * 2:2], mixed[1:amount // 2 * 2:2]
    margin = jnp.minimum(tallies[giver] - 1, reach - tallies[sink]) // 2
    margin = jnp.where((giver == order[0]) | (sink == order[0]) | (tallies[sink] == 0), 0, jnp.maximum(margin, 0))
    passed = jax.random.randint(jax.random.fold_in(own, 4), (amount // 2,), 0, 1 << 20) % (margin + 1)
    tallies = tallies.at[giver].add(-passed).at[sink].add(passed)
    items = jnp.searchsorted(jnp.cumsum(tallies), jnp.arange(rows * top), side="right").astype(jnp.int32)
    table = items.reshape(top, rows).T
    table = table[jax.random.permutation(jax.random.fold_in(own, 1), rows)]
    offset_by = jax.random.randint(jax.random.fold_in(own, 2), (rows, 1), 0, top)
    return jnp.take_along_axis(table, (jnp.arange(top)[None, :] + offset_by) % top, axis=1)


def shares(amount, total, most, lean, full):
    portions = [(1 << 20) // math.isqrt(standing ** lean) + 1 for standing in range(1, amount + 1)]
    largest = most if full else min(most, max(-(-total // amount), total * portions[0] // sum(portions)))
    least = 1 if total - largest >= amount - 1 else 0
    counts, rest = [largest] + [least] * (amount - 1), total - largest - least * (amount - 1)
    while rest > 0:
        free = [i for i in range(1, amount) if counts[i] < largest] or [i for i in range(1, amount) if counts[i] < most]
        whole, left = sum([portions[i] for i in free]), rest
        for i in free:
            extra = min(most - counts[i], max(1, left * portions[i] // whole), rest)
            counts[i] = counts[i] + extra
            rest = rest - extra
    return np.array(counts)


def normal_values(rng, dims, spread, most, split=(), kind=jnp.bfloat16):
    entries = spread * jax.random.normal(rng, dims, jnp.float32)
    if split:
        entries = entries * level_of(rng, dims, split, -0.22, 0.18)
    return jnp.clip(entries, -most, most).astype(kind)


def setup_inputs(seed: int = 0) -> dict:
    arg_keys = jax.random.split(jax.random.key(seed), 7)
    tokens = normal_values(arg_keys[0], (TOKENS, D), 1.0, 6.0, ((0, 32),))
    out_grad = normal_values(arg_keys[1], (TOKENS, D), 1.0, 6.0, ((0, 32),))
    gate = jnp.clip(0.2 + 0.8 * jax.random.uniform(arg_keys[2], (TOKENS,), jnp.float32) ** level_of(arg_keys[2], (TOKENS,), ((0, 32),), -0.2, 0.2), 0.2, 1.0)
    region_keys = jax.random.split(jax.random.fold_in(arg_keys[3], 1), TOKENS // TOK_DEV)
    region_turns = jax.random.permutation(jax.random.fold_in(arg_keys[3], 3), TOKENS // TOK_DEV)
    region = jax.vmap(lambda own, number: routed_block(jax.random.fold_in(arg_keys[3], 2), own, number, TOK_DEV, EXPERTS, 1, CAP, 2))(region_keys, region_turns).reshape((TOKENS, 1))
    w_in = normal_values(arg_keys[4], (EXPERTS, FF, D), D ** -0.5, 0.1875, ((0, 4),))
    w_out = normal_values(arg_keys[5], (EXPERTS, FF, D), FF ** -0.5, 0.09375, ((0, 4),))
    return {"tokens": tokens, "out_grad": out_grad, "gate": gate, "region": region, "w_in": w_in, "w_out": w_out}


def gelu_parts(pre_act):
    root_two_pi = 0.7978845608028654
    cubic = pre_act * pre_act * pre_act
    tanh_val = jnp.tanh(root_two_pi * (pre_act + 0.044715 * cubic))
    halved = 0.5 * (1.0 + tanh_val)
    gelu_value = pre_act * halved
    gelu_slope = halved + 0.5 * pre_act * (1.0 - tanh_val * tanh_val) * root_two_pi * (1.0 + 3.0 * 0.044715 * pre_act * pre_act)
    return (gelu_value, gelu_slope)

def reference(tokens, out_grad, gate, region, w_in, w_out):
    scaled = (gate[:, None] * out_grad.astype(jnp.float32)).astype(jnp.bfloat16)
    region_ids = region[:, 0].astype(jnp.int32)
    block_len = N_EXPERT * TOK_DEV
    window_rows = N_EXPERT * CAP
    grad_scale = 1.0 / math.sqrt(float(TOKENS // EXPERTS))

    def one_expert(running, expert_id):
        weight_in = w_in[expert_id]
        weight_out = w_out[expert_id]

        def one_group(carry, group_id):
            tok_acc, acc_in, acc_out = carry
            base = (group_id * block_len).astype(jnp.int32)
            block_ids = lax.dynamic_slice(region_ids, (base,), (block_len,))
            local_order = jnp.argsort(block_ids, stable=True).astype(jnp.int32)
            count = jnp.sum((block_ids == expert_id).astype(jnp.int32)).astype(jnp.int32)
            start = jnp.sum((block_ids < expert_id).astype(jnp.int32)).astype(jnp.int32)
            order_pad = jnp.concatenate([local_order, jnp.zeros((window_rows,), jnp.int32)]).astype(jnp.int32)
            picked = (lax.dynamic_slice(order_pad, (start,), (window_rows,)) + base).astype(jnp.int32)
            is_kept = (jnp.arange(window_rows, dtype=jnp.int32) < count)[:, None]
            inputs_win = jnp.where(is_kept, tokens[picked], jnp.zeros((), tokens.dtype))
            grads_win = jnp.where(is_kept, scaled[picked], jnp.zeros((), scaled.dtype))
            pre_act = lax.dot_general(inputs_win, weight_in, (((1,), (1,)), ((), ())), preferred_element_type=jnp.float32)
            gelu_value, gelu_slope = gelu_parts(pre_act)
            activation = gelu_value.astype(jnp.bfloat16)
            act_grad = lax.dot_general(grads_win, weight_out, (((1,), (1,)), ((), ())), preferred_element_type=jnp.float32)
            pre_grad = (act_grad * gelu_slope).astype(jnp.bfloat16)
            row_grads = jnp.dot(pre_grad, weight_in, preferred_element_type=jnp.float32).astype(jnp.bfloat16)
            part_in = lax.dot_general(pre_grad, inputs_win, (((0,), (0,)), ((), ())), preferred_element_type=jnp.float32).astype(jnp.bfloat16)
            part_out = lax.dot_general(activation, grads_win, (((0,), (0,)), ((), ())), preferred_element_type=jnp.float32).astype(jnp.bfloat16)
            tok_acc = tok_acc.at[picked].add(jnp.where(is_kept, row_grads, jnp.zeros((), row_grads.dtype)))
            acc_in = acc_in + part_in.astype(jnp.float32)
            acc_out = acc_out + part_out.astype(jnp.float32)
            return ((tok_acc, acc_in, acc_out), None)
        zeros_grad = jnp.zeros((FF, D), jnp.float32)
        (running, acc_in, acc_out), unused = lax.scan(one_group, (running, zeros_grad, zeros_grad), jnp.arange(N_DP, dtype=jnp.int32))
        return (running, (acc_in * grad_scale, acc_out * grad_scale))
    token_grad, (w_in_grad, w_out_grad) = lax.scan(one_expert, jnp.zeros(tokens.shape, jnp.bfloat16), jnp.arange(EXPERTS, dtype=jnp.int32))
    return (token_grad, w_in_grad, w_out_grad)
```

```python
import math

import jax
import jax.numpy as jnp
from jax import lax
from jax.experimental import pallas as pl
from jax.experimental.pallas import tpu as pltpu
from jax.sharding import PartitionSpec as P


MESH = pl.DeviceIdType.MESH
NT = (((1,), (1,)), ((), ()))


def gelu_halves(p):
    c = 0.7978845608028654
    square = p * p
    h = 0.5 + 0.5 * jnp.tanh(p * (c + (c * 0.044715) * square))
    value = p * h
    slope = h + value * (1.0 - h) * (2.0 * c + (6.0 * c * 0.044715) * square)
    return value, slope


def gelu_parts(pre_act):
    root_two_pi = 0.7978845608028654
    cubic = pre_act * pre_act * pre_act
    tanh_val = jnp.tanh(root_two_pi * (pre_act + 0.044715 * cubic))
    halved = 0.5 * (1.0 + tanh_val)
    gelu_value = pre_act * halved
    gelu_slope = halved + 0.5 * pre_act * (1.0 - tanh_val * tanh_val) * root_two_pi * (
        1.0 + 3.0 * 0.044715 * pre_act * pre_act
    )
    return (gelu_value, gelu_slope)


def expert_rows(inputs_win, grads_win, weight_in, weight_out):
    pre_act = lax.dot_general(
        inputs_win, weight_in, (((1,), (1,)), ((), ())), preferred_element_type=jnp.float32
    )
    gelu_value, gelu_slope = gelu_parts(pre_act)
    activation = gelu_value.astype(jnp.bfloat16)
    act_grad = lax.dot_general(
        grads_win, weight_out, (((1,), (1,)), ((), ())), preferred_element_type=jnp.float32
    )
    pre_grad = (act_grad * gelu_slope).astype(jnp.bfloat16)
    row_grads = jnp.dot(pre_grad, weight_in, preferred_element_type=jnp.float32).astype(
        jnp.bfloat16
    )
    return (activation, pre_grad, row_grads)


def send_back(row_grads):
    return lax.all_to_all(row_grads, "expert", split_axis=0, concat_axis=0, tiled=True)


def local(tokens, out_grad, gate, region, w_in, w_out):
    groups = lax.axis_size("expert")
    dp_count = lax.axis_size("dp")
    token_count = tokens.shape[0]
    model_width = tokens.shape[1]
    capacity = 2 * token_count // groups
    slot_count = groups * capacity
    region_ids = region[:, 0]
    onehot = (region_ids[:, None] == jnp.arange(groups, dtype=jnp.int32)[None, :]).astype(jnp.int32)
    rank_in = jnp.sum(jnp.cumsum(onehot, 0) * onehot, 1) - 1
    slot_ids = region_ids * capacity + rank_in
    scaled = (gate[:, None] * out_grad.astype(jnp.float32)).astype(jnp.bfloat16)
    send_x = jnp.zeros((slot_count, model_width), jnp.bfloat16).at[slot_ids].set(tokens)
    send_d = jnp.zeros((slot_count, model_width), jnp.bfloat16).at[slot_ids].set(scaled)
    recv_x, recv_d = (
        lax.all_to_all(send_x, "expert", split_axis=0, concat_axis=0, tiled=True),
        lax.all_to_all(send_d, "expert", split_axis=0, concat_axis=0, tiled=True),
    )
    weight_in = w_in[0]
    weight_out = w_out[0]
    activation, pre_grad, row_grads = expert_rows(recv_x, recv_d, weight_in, weight_out)
    grad_scale = 1.0 / math.sqrt(float(token_count * dp_count))
    returned = send_back(row_grads)
    summed = lax.psum_scatter(
        jnp.concatenate(
            [
                lax.dot_general(
                    pre_grad, recv_x, (((0,), (0,)), ((), ())), preferred_element_type=jnp.float32
                ),
                lax.dot_general(
                    activation, recv_d, (((0,), (0,)), ((), ())), preferred_element_type=jnp.float32
                ),
            ],
            axis=1,
        ).astype(jnp.bfloat16),
        "dp",
        scatter_dimension=0,
        tiled=True,
    ).astype(jnp.float32)
    grad_in = summed[:, :model_width]
    grad_out = summed[:, model_width:]
    token_grad = returned[slot_ids]
    return (token_grad, (grad_in * grad_scale)[None], (grad_out * grad_scale)[None])


def routed_kernel(
    tokens_ref, out_grad_ref, gate_ref, region_ref, w_in_hbm, w_out_hbm,
    token_grad_ref, grad_in_ref, grad_out_ref,
    rows, outbox, weight_in, weight_out, perm_back, row_grads, returned,
    recv_sem, own_sem, pair_sem, fwd_sem, z_sem, back_send_sem, back_recv_sem, weight_sem,
):
    dp = lax.axis_index("dp")
    z = lax.axis_index("expert")
    core = dp % 2
    chip = dp // 2
    cx = chip % 2
    cy = chip // 2
    pair = dp + 1 - 2 * core
    along_x = (cy * 2 + 1 - cx) * 2 + core
    along_y = ((1 - cy) * 2 + cx) * 2 + core
    forward_to = along_y * (1 - core) + along_x * core
    peers = [z, z + 1 - 2 * (z % 2), (z + 2) % 4, 3 - z]
    tok = tokens_ref.shape[0]
    cap = rows.shape[3] // 2
    f_own = grad_in_ref.shape[0]

    def half(q, r, k, c):
        return rows.at[q, r, k, pl.ds(pl.multiple_of(c * cap, cap), cap)]

    def remote(src, dst, send, recv, where):
        return pltpu.make_async_remote_copy(
            src_ref=src, dst_ref=dst, send_sem=send, recv_sem=recv, device_id=where, device_id_type=MESH
        )

    def arrival(q, r, k, c):
        slot = half(q, r, k, c)
        return remote(slot, slot, own_sem.at[q, r, 0], recv_sem.at[q, r, k, c], (pair, z))

    def own_copies(q, r):
        src = half(q, r, 0, core)
        return [
            remote(src, half(q, r, 1, core), own_sem.at[q, r, 0], recv_sem.at[q, r, 1, core], (along_x, z)),
            remote(src, half(q, r, 2, core), own_sem.at[q, r, 1], recv_sem.at[q, r, 2, core], (along_y, z)),
            remote(src, half(q, r, 0, core), own_sem.at[q, r, 2], recv_sem.at[q, r, 0, core], (pair, z)),
        ]

    def forward_copy(q, r):
        return remote(
            half(q, r, 1 + core, core), half(q, r, 3, core), fwd_sem.at[q, r], recv_sem.at[q, r, 3, core], (forward_to, z)
        )

    def pair_copy(q, r, k):
        slot = half(q, r, k, core)
        return remote(slot, slot, pair_sem.at[q, r, k - 1], recv_sem.at[q, r, k, core], (pair, z))

    def z_copy(q, r):
        return remote(outbox.at[q, r - 1], half(q, r, 0, core), z_sem.at[q, r - 1], recv_sem.at[q, r, 0, core], (dp, peers[r]))

    def back_copy(r):
        return remote(
            row_grads.at[r], returned.at[r], back_send_sem.at[r - 1], back_recv_sem.at[r - 1], (dp, peers[r])
        )

    weight_copies = [
        pltpu.make_async_copy(w_in_hbm, weight_in, weight_sem.at[0]),
        pltpu.make_async_copy(w_out_hbm, weight_out, weight_sem.at[1]),
    ]
    for copy in weight_copies:
        copy.start()
    barrier = pltpu.get_barrier_semaphore()
    for where in [(pair, z), (along_x, z), (along_y, z)] + [(dp, peer) for peer in peers[1:]]:
        pl.semaphore_signal(barrier, inc=1, device_id=where, device_id_type=MESH)

    region = region_ref[...]
    onehot = (jnp.broadcast_to(region, (8, tok)) == lax.broadcasted_iota(jnp.int32, (8, tok), 0)).astype(jnp.float32)
    upto = lax.broadcasted_iota(jnp.int32, (tok, tok), 0) <= lax.broadcasted_iota(jnp.int32, (tok, tok), 1)
    counts = jnp.dot(
        onehot.astype(jnp.bfloat16), upto.astype(jnp.float32).astype(jnp.bfloat16), preferred_element_type=jnp.float32
    )
    rank = jnp.sum(onehot * counts, axis=0, keepdims=True) - 1.0
    slot_ids = region * cap + rank.astype(jnp.int32)
    places = lax.broadcasted_iota(jnp.int32, (cap, tok), 0)
    gates = jnp.broadcast_to(gate_ref[...], (cap, tok))

    def route(r):
        here = (places + peers[r] * cap) == slot_ids
        moved = here.astype(jnp.float32)
        perm_back[:, r * cap : (r + 1) * cap] = moved.T.astype(jnp.bfloat16)
        moved = moved.astype(jnp.bfloat16)
        gate_rows = jnp.sum(jnp.where(here, gates, 0.0), axis=1, keepdims=True)
        inputs = jnp.dot(moved, tokens_ref[...], preferred_element_type=jnp.float32).astype(jnp.bfloat16)
        grads = jnp.dot(moved, out_grad_ref[...], preferred_element_type=jnp.float32)
        return inputs, (gate_rows * grads).astype(jnp.bfloat16)

    for r in (1, 2, 3):
        inputs, grads = route(r)
        outbox[0, r - 1] = inputs
        outbox[1, r - 1] = grads
    inputs, grads = route(0)
    mine = pl.ds(pl.multiple_of(core * cap, cap), cap)
    rows[0, 0, 0, mine] = inputs
    rows[1, 0, 0, mine] = grads

    pl.semaphore_wait(barrier, 6)
    for q, r in ((0, 1), (0, 2), (1, 1), (1, 2), (0, 3), (1, 3)):
        z_copy(q, r).start()
    for q in (0, 1):
        for copy in own_copies(q, 0):
            copy.start()
    grad_in_ref[...] = jnp.zeros_like(grad_in_ref)
    grad_out_ref[...] = jnp.zeros_like(grad_out_ref)
    for copy in weight_copies:
        copy.wait()
    own_f = pl.ds(pl.multiple_of(dp * f_own, f_own), f_own)

    def weight_grads(r, k):
        for q in (0, 1):
            arrival(q, r, k, 1 - core).wait_recv()
        inputs = rows[0, r, k]
        grads = rows[1, r, k]
        pre_act = lax.dot_general(weight_in[own_f], inputs, NT, preferred_element_type=jnp.float32)
        act_grad = lax.dot_general(weight_out[own_f], grads, NT, preferred_element_type=jnp.float32)
        value, slope = gelu_halves(pre_act)
        activation = value.astype(jnp.bfloat16)
        pre_grad = (act_grad * slope).astype(jnp.bfloat16)
        grad_in_ref[...] += jnp.dot(pre_grad, inputs, preferred_element_type=jnp.float32)
        grad_out_ref[...] += jnp.dot(activation, grads, preferred_element_type=jnp.float32)

    def input_grads(r):
        inputs = jnp.concatenate([rows[0, r - 1, 0, mine], rows[0, r, 0, mine]], axis=0)
        grads = jnp.concatenate([rows[1, r - 1, 0, mine], rows[1, r, 0, mine]], axis=0)

        def part(i, total):
            chunk = pl.ds(pl.multiple_of(i * 512, 512), 512)
            w = weight_in[chunk]
            pre_act = lax.dot_general(inputs, w, NT, preferred_element_type=jnp.float32)
            act_grad = lax.dot_general(grads, weight_out[chunk], NT, preferred_element_type=jnp.float32)
            pre_grad = (act_grad * gelu_halves(pre_act)[1]).astype(jnp.bfloat16)
            return total + jnp.dot(pre_grad, w, preferred_element_type=jnp.float32)

        total = lax.fori_loop(0, weight_in.shape[0] // 512, part, jnp.zeros((2 * cap, tokens_ref.shape[1]), jnp.float32))
        row_grads[r - 1] = total[:cap].astype(jnp.bfloat16)
        row_grads[r] = total[cap:].astype(jnp.bfloat16)

    def one_round(r, carry):
        @pl.when(r % 2 == 1)
        def _():
            input_grads(r)

        @pl.when(r == 1)
        def _():
            back_copy(1).start()

        @pl.when(r == 3)
        def _():
            back_copy(2).start()
            back_copy(3).start()

        def early(j, carry):
            weight_grads(r - j, 3 * j)
            return carry

        lax.fori_loop(0, jnp.where(r == 0, 1, 2), early, 0)
        for q in (0, 1):
            for k in (1, 2):
                arrival(q, r, k, core).wait_recv()
            forward_copy(q, r).start()
            for k in (1, 2):
                pair_copy(q, r, k).start()

        @pl.when(r < 3)
        def _():
            for q in (0, 1):
                arrival(q, r + 1, 0, core).wait_recv()
                for copy in own_copies(q, r + 1):
                    copy.start()

        def late(k, carry):
            weight_grads(r, k)
            return carry

        lax.fori_loop(1, 3, late, 0)
        for q in (0, 1):
            arrival(q, r, 3, core).wait_recv()
            pair_copy(q, r, 3).start()
        return carry

    lax.fori_loop(0, 4, one_round, 0)
    weight_grads(3, 3)
    returned[0] = row_grads[0]
    for r in (1, 2, 3):
        back_copy(r).wait_recv()
    collected = returned[...].reshape(4 * cap, tokens_ref.shape[1])
    token_grad_ref[...] = jnp.dot(perm_back[...], collected, preferred_element_type=jnp.float32).astype(jnp.bfloat16)

    for r in (1, 2, 3):
        back_copy(r).wait_send()
        for q in (0, 1):
            z_copy(q, r).wait_send()

    def drain(r, carry):
        for q in (0, 1):
            for copy in own_copies(q, r):
                copy.wait_send()
            forward_copy(q, r).wait_send()
            for k in (1, 2, 3):
                pair_copy(q, r, k).wait_send()
        return carry

    lax.fori_loop(0, 4, drain, 0)


def routed_local(tokens, out_grad, gate, region, w_in, w_out):
    dp_count = lax.axis_size("dp")
    tok, width = tokens.shape
    cap = tok // 2
    hidden = w_in.shape[1]
    f_own = hidden // dp_count
    vmem = pl.BlockSpec(memory_space=pltpu.VMEM)
    hbm = pl.BlockSpec(memory_space=pl.ANY)
    dma = pltpu.SemaphoreType.DMA
    token_grad, grad_in, grad_out = pl.pallas_call(
        routed_kernel,
        out_shape=(
            jax.ShapeDtypeStruct((tok, width), jnp.bfloat16),
            jax.ShapeDtypeStruct((f_own, width), jnp.float32),
            jax.ShapeDtypeStruct((f_own, width), jnp.float32),
        ),
        in_specs=[vmem, vmem, vmem, vmem, hbm, hbm],
        out_specs=(vmem, vmem, vmem),
        scratch_shapes=[
            pltpu.VMEM((2, 4, 4, 2 * cap, width), jnp.bfloat16),
            pltpu.VMEM((2, 3, cap, width), jnp.bfloat16),
            pltpu.VMEM((hidden, width), jnp.bfloat16),
            pltpu.VMEM((hidden, width), jnp.bfloat16),
            pltpu.VMEM((tok, 4 * cap), jnp.bfloat16),
            pltpu.VMEM((4, cap, width), jnp.bfloat16),
            pltpu.VMEM((4, cap, width), jnp.bfloat16),
            dma((2, 4, 4, 2)),
            dma((2, 4, 3)),
            dma((2, 4, 3)),
            dma((2, 4)),
            dma((2, 3)),
            dma((3,)),
            dma((3,)),
            dma((2,)),
        ],
        compiler_params=pltpu.CompilerParams(
            collective_id=0, has_side_effects=True, vmem_limit_bytes=58 * 1024 * 1024
        ),
        cost_estimate=pl.CostEstimate(
            flops=14 * 4 * cap * hidden * width, bytes_accessed=4 * hidden * width + 8 * f_own * width, transcendentals=8 * cap * hidden
        ),
    )(tokens, out_grad, gate.reshape(1, tok), region.reshape(1, tok), w_in[0], w_out[0])
    grad_scale = 1.0 / math.sqrt(float(tok * dp_count))
    return (token_grad, (grad_in * grad_scale)[None], (grad_out * grad_scale)[None])


def solution(mesh):
    small = mesh.shape["dp"] == 8 and mesh.shape["expert"] == 4
    return jax.shard_map(
        routed_local if small else local,
        mesh=mesh,
        in_specs=(
            P(("dp", "expert"), None),
            P(("dp", "expert"), None),
            P(("dp", "expert")),
            P(("dp", "expert"), None),
            P("expert", None, None),
            P("expert", None, None),
        ),
        out_specs=(P(("dp", "expert"), None), P("expert", "dp", None), P("expert", "dp", None)),
        check_vma=False,
    )
```

```python
import math

import jax
import jax.numpy as jnp
from jax import lax
from jax.experimental import pallas as pl
from jax.experimental.pallas import tpu as pltpu
from jax.sharding import PartitionSpec as P


MESH = pl.DeviceIdType.MESH
NT = (((1,), (1,)), ((), ()))
STEPS = [(0, 0, 1, 0), (0, 1, 0, 2), (1, 1, 1, 2), (0, 3, 1, 3), (2, 0, 3, 0), (2, 1, 2, 2), (3, 1, 3, 2)]


def gelu_halves(p):
    c = 0.7978845608028654
    square = p * p
    h = 0.5 + 0.5 * jnp.tanh(p * (c + (c * 0.044715) * square))
    value = p * h
    slope = h + value * (1.0 - h) * (2.0 * c + (6.0 * c * 0.044715) * square)
    return value, slope


def gelu_parts(pre_act):
    root_two_pi = 0.7978845608028654
    cubic = pre_act * pre_act * pre_act
    tanh_val = jnp.tanh(root_two_pi * (pre_act + 0.044715 * cubic))
    halved = 0.5 * (1.0 + tanh_val)
    gelu_value = pre_act * halved
    gelu_slope = halved + 0.5 * pre_act * (1.0 - tanh_val * tanh_val) * root_two_pi * (
        1.0 + 3.0 * 0.044715 * pre_act * pre_act
    )
    return (gelu_value, gelu_slope)


def expert_rows(inputs_win, grads_win, weight_in, weight_out):
    pre_act = lax.dot_general(
        inputs_win, weight_in, (((1,), (1,)), ((), ())), preferred_element_type=jnp.float32
    )
    gelu_value, gelu_slope = gelu_parts(pre_act)
    activation = gelu_value.astype(jnp.bfloat16)
    act_grad = lax.dot_general(
        grads_win, weight_out, (((1,), (1,)), ((), ())), preferred_element_type=jnp.float32
    )
    pre_grad = (act_grad * gelu_slope).astype(jnp.bfloat16)
    row_grads = jnp.dot(pre_grad, weight_in, preferred_element_type=jnp.float32).astype(
        jnp.bfloat16
    )
    return (activation, pre_grad, row_grads)


def send_back(row_grads):
    return lax.all_to_all(row_grads, "expert", split_axis=0, concat_axis=0, tiled=True)


def local(tokens, out_grad, gate, region, w_in, w_out):
    groups = lax.axis_size("expert")
    dp_count = lax.axis_size("dp")
    token_count = tokens.shape[0]
    model_width = tokens.shape[1]
    capacity = 2 * token_count // groups
    slot_count = groups * capacity
    region_ids = region[:, 0]
    onehot = (region_ids[:, None] == jnp.arange(groups, dtype=jnp.int32)[None, :]).astype(jnp.int32)
    rank_in = jnp.sum(jnp.cumsum(onehot, 0) * onehot, 1) - 1
    slot_ids = region_ids * capacity + rank_in
    scaled = (gate[:, None] * out_grad.astype(jnp.float32)).astype(jnp.bfloat16)
    send_x = jnp.zeros((slot_count, model_width), jnp.bfloat16).at[slot_ids].set(tokens)
    send_d = jnp.zeros((slot_count, model_width), jnp.bfloat16).at[slot_ids].set(scaled)
    recv_x, recv_d = (
        lax.all_to_all(send_x, "expert", split_axis=0, concat_axis=0, tiled=True),
        lax.all_to_all(send_d, "expert", split_axis=0, concat_axis=0, tiled=True),
    )
    weight_in = w_in[0]
    weight_out = w_out[0]
    activation, pre_grad, row_grads = expert_rows(recv_x, recv_d, weight_in, weight_out)
    grad_scale = 1.0 / math.sqrt(float(token_count * dp_count))
    returned = send_back(row_grads)
    summed = lax.psum_scatter(
        jnp.concatenate(
            [
                lax.dot_general(
                    pre_grad, recv_x, (((0,), (0,)), ((), ())), preferred_element_type=jnp.float32
                ),
                lax.dot_general(
                    activation, recv_d, (((0,), (0,)), ((), ())), preferred_element_type=jnp.float32
                ),
            ],
            axis=1,
        ).astype(jnp.bfloat16),
        "dp",
        scatter_dimension=0,
        tiled=True,
    ).astype(jnp.float32)
    grad_in = summed[:, :model_width]
    grad_out = summed[:, model_width:]
    token_grad = returned[slot_ids]
    return (token_grad, (grad_in * grad_scale)[None], (grad_out * grad_scale)[None])


def routed_kernel(
    tokens_ref, out_grad_ref, gate_ref, region_ref, w_in_hbm, w_out_hbm,
    token_grad_ref, grad_in_ref, grad_out_ref,
    rows, outbox, weight_in, weight_out, perm_back, row_grads, returned,
    recv_sem, own_sem, pair_sem, fwd_sem, z_sem, back_send_sem, back_recv_sem, weight_sem,
):
    dp = lax.axis_index("dp")
    z = lax.axis_index("expert")
    core = dp % 2
    chip = dp // 2
    cx = chip % 2
    cy = chip // 2
    pair = dp + 1 - 2 * core
    along_x = (cy * 2 + 1 - cx) * 2 + core
    along_y = ((1 - cy) * 2 + cx) * 2 + core
    forward_to = along_y * (1 - core) + along_x * core
    peers = [z, z + 1 - 2 * (z % 2), (z + 2) % 4, 3 - z]
    tok = tokens_ref.shape[0]
    cap = rows.shape[3] // 2
    f_own = grad_in_ref.shape[0]

    def half(q, r, k, c):
        return rows.at[q, r, k, pl.ds(pl.multiple_of(c * cap, cap), cap)]

    def remote(src, dst, send, recv, where):
        return pltpu.make_async_remote_copy(
            src_ref=src, dst_ref=dst, send_sem=send, recv_sem=recv, device_id=where, device_id_type=MESH
        )

    def arrival(q, r, k, c):
        slot = half(q, r, k, c)
        return remote(slot, slot, own_sem.at[q, r, 0], recv_sem.at[q, r, k, c], (pair, z))

    def own_copies(q, r):
        src = half(q, r, 0, core)
        return [
            remote(src, half(q, r, 1, core), own_sem.at[q, r, 0], recv_sem.at[q, r, 1, core], (along_x, z)),
            remote(src, half(q, r, 2, core), own_sem.at[q, r, 1], recv_sem.at[q, r, 2, core], (along_y, z)),
            remote(src, half(q, r, 0, core), own_sem.at[q, r, 2], recv_sem.at[q, r, 0, core], (pair, z)),
        ]

    def forward_copy(q, r):
        return remote(
            half(q, r, 1 + core, core), half(q, r, 3, core), fwd_sem.at[q, r], recv_sem.at[q, r, 3, core], (forward_to, z)
        )

    def pair_copy(q, r, k):
        slot = half(q, r, k, core)
        return remote(slot, slot, pair_sem.at[q, r, k - 1], recv_sem.at[q, r, k, core], (pair, z))

    def z_copy(q, r):
        return remote(outbox.at[q, r - 1], half(q, r, 0, core), z_sem.at[q, r - 1], recv_sem.at[q, r, 0, core], (dp, peers[r]))

    def back_copy(r):
        return remote(
            row_grads.at[r], returned.at[r], back_send_sem.at[r - 1], back_recv_sem.at[r - 1], (dp, peers[r])
        )

    weight_copies = [
        pltpu.make_async_copy(w_in_hbm, weight_in, weight_sem.at[0]),
        pltpu.make_async_copy(w_out_hbm, weight_out, weight_sem.at[1]),
    ]
    for copy in weight_copies:
        copy.start()
    barrier = pltpu.get_barrier_semaphore()
    for where in [(pair, z), (along_x, z), (along_y, z)] + [(dp, peer) for peer in peers[1:]]:
        pl.semaphore_signal(barrier, inc=1, device_id=where, device_id_type=MESH)

    region = region_ref[...]
    onehot = (jnp.broadcast_to(region, (8, tok)) == lax.broadcasted_iota(jnp.int32, (8, tok), 0)).astype(jnp.float32)
    upto = lax.broadcasted_iota(jnp.int32, (tok, tok), 0) <= lax.broadcasted_iota(jnp.int32, (tok, tok), 1)
    counts = jnp.dot(
        onehot.astype(jnp.bfloat16), upto.astype(jnp.float32).astype(jnp.bfloat16), preferred_element_type=jnp.float32
    )
    rank = jnp.sum(onehot * counts, axis=0, keepdims=True) - 1.0
    slot_ids = region * cap + rank.astype(jnp.int32)
    places = lax.broadcasted_iota(jnp.int32, (cap, tok), 0)
    gates = jnp.broadcast_to(gate_ref[...], (cap, tok))

    def route(r):
        here = (places + peers[r] * cap) == slot_ids
        moved = here.astype(jnp.float32)
        perm_back[:, r * cap : (r + 1) * cap] = moved.T.astype(jnp.bfloat16)
        moved = moved.astype(jnp.bfloat16)
        gate_rows = jnp.sum(jnp.where(here, gates, 0.0), axis=1, keepdims=True)
        inputs = jnp.dot(moved, tokens_ref[...], preferred_element_type=jnp.float32).astype(jnp.bfloat16)
        grads = jnp.dot(moved, out_grad_ref[...], preferred_element_type=jnp.float32)
        return inputs, (gate_rows * grads).astype(jnp.bfloat16)

    for r in (1, 2, 3):
        inputs, grads = route(r)
        outbox[0, r - 1] = inputs
        outbox[1, r - 1] = grads
    inputs, grads = route(0)
    mine = pl.ds(pl.multiple_of(core * cap, cap), cap)
    rows[0, 0, 0, mine] = inputs
    rows[1, 0, 0, mine] = grads

    pl.semaphore_wait(barrier, 6)
    for q, r in ((0, 1), (0, 2), (1, 1), (1, 2), (0, 3), (1, 3)):
        z_copy(q, r).start()
    for q in (0, 1):
        for copy in own_copies(q, 0):
            copy.start()
    grad_in_ref[...] = jnp.zeros_like(grad_in_ref)
    grad_out_ref[...] = jnp.zeros_like(grad_out_ref)
    for copy in weight_copies:
        copy.wait()
    own_f = pl.ds(pl.multiple_of(dp * f_own, f_own), f_own)

    def weight_grads(places):
        for r, k in places:
            for q in (0, 1):
                arrival(q, r, k, 1 - core).wait_recv()
        inputs = jnp.concatenate([rows[0, r, k] for r, k in places], axis=0)
        grads = jnp.concatenate([rows[1, r, k] for r, k in places], axis=0)
        pre_act = lax.dot_general(weight_in[own_f], inputs, NT, preferred_element_type=jnp.float32)
        act_grad = lax.dot_general(weight_out[own_f], grads, NT, preferred_element_type=jnp.float32)
        value, slope = gelu_halves(pre_act)
        activation = value.astype(jnp.bfloat16)
        pre_grad = (act_grad * slope).astype(jnp.bfloat16)
        grad_in_ref[...] += jnp.dot(pre_grad, inputs, preferred_element_type=jnp.float32)
        grad_out_ref[...] += jnp.dot(activation, grads, preferred_element_type=jnp.float32)

    def input_grads(rounds):
        inputs = jnp.concatenate([rows[0, r, 0, mine] for r in rounds], axis=0)
        grads = jnp.concatenate([rows[1, r, 0, mine] for r in rounds], axis=0)

        def part(i, total):
            chunk = pl.ds(pl.multiple_of(i * 512, 512), 512)
            w = weight_in[chunk]
            pre_act = lax.dot_general(inputs, w, NT, preferred_element_type=jnp.float32)
            act_grad = lax.dot_general(grads, weight_out[chunk], NT, preferred_element_type=jnp.float32)
            pre_grad = (act_grad * gelu_halves(pre_act)[1]).astype(jnp.bfloat16)
            return total + jnp.dot(pre_grad, w, preferred_element_type=jnp.float32)

        zeros = jnp.zeros((len(rounds) * cap, tokens_ref.shape[1]), jnp.float32)
        total = lax.fori_loop(0, weight_in.shape[0] // 512, part, zeros).astype(jnp.bfloat16)
        for i, r in enumerate(rounds):
            row_grads[r] = total[i * cap : (i + 1) * cap]

    def from_z(r):
        for q in (0, 1):
            arrival(q, r, 0, core).wait_recv()
            for copy in own_copies(q, r):
                copy.start()

    def from_sides(r):
        for q in (0, 1):
            for k in (1, 2):
                arrival(q, r, k, core).wait_recv()
            forward_copy(q, r).start()
            for k in (1, 2):
                pair_copy(q, r, k).start()

    def from_diagonal(r):
        for q in (0, 1):
            arrival(q, r, 3, core).wait_recv()
            pair_copy(q, r, 3).start()

    def step(s, table):
        @pl.when((s == 0) | (s == 3) | (s == 4))
        def _():
            from_z(lax.max(s - 1, 1))

        @pl.when(s == 3)
        def _():
            input_grads((1, 2))
            back_copy(1).start()
            back_copy(2).start()
            from_diagonal(0)
            from_diagonal(1)

        @pl.when(s == 4)
        def _():
            input_grads((3,))
            back_copy(3).start()

        @pl.when((s == 1) | (s == 2) | (s == 5) | (s == 6))
        def _():
            from_sides(s - 1 - 2 * (s // 5))

        r1, k1, r2, k2 = [column % 4 for column in table]
        weight_grads([(r1, k1), (r2, k2)])
        return tuple(column // 4 for column in table)

    input_grads((0,))
    table = [0, 0, 0, 0]
    for s, entry in enumerate(STEPS):
        for i, digit in enumerate(entry):
            table[i] += digit * 4**s
    lax.fori_loop(0, len(STEPS), step, tuple(jnp.int32(column) for column in table))

    def last(r, carry):
        from_diagonal(r)
        weight_grads([(r, 3)])
        return carry

    lax.fori_loop(2, 4, last, 0)
    returned[0] = row_grads[0]
    for r in (1, 2, 3):
        back_copy(r).wait_recv()
    collected = returned[...].reshape(4 * cap, tokens_ref.shape[1])
    token_grad_ref[...] = jnp.dot(perm_back[...], collected, preferred_element_type=jnp.float32).astype(jnp.bfloat16)

    for r in (1, 2, 3):
        back_copy(r).wait_send()
        for q in (0, 1):
            z_copy(q, r).wait_send()

    def drain(r, carry):
        for q in (0, 1):
            for copy in own_copies(q, r):
                copy.wait_send()
            forward_copy(q, r).wait_send()
            for k in (1, 2, 3):
                pair_copy(q, r, k).wait_send()
        return carry

    lax.fori_loop(0, 4, drain, 0)


def routed_local(tokens, out_grad, gate, region, w_in, w_out):
    dp_count = lax.axis_size("dp")
    tok, width = tokens.shape
    cap = tok // 2
    hidden = w_in.shape[1]
    f_own = hidden // dp_count
    vmem = pl.BlockSpec(memory_space=pltpu.VMEM)
    hbm = pl.BlockSpec(memory_space=pl.ANY)
    dma = pltpu.SemaphoreType.DMA
    token_grad, grad_in, grad_out = pl.pallas_call(
        routed_kernel,
        out_shape=(
            jax.ShapeDtypeStruct((tok, width), jnp.bfloat16),
            jax.ShapeDtypeStruct((f_own, width), jnp.float32),
            jax.ShapeDtypeStruct((f_own, width), jnp.float32),
        ),
        in_specs=[vmem, vmem, vmem, vmem, hbm, hbm],
        out_specs=(vmem, vmem, vmem),
        scratch_shapes=[
            pltpu.VMEM((2, 4, 4, 2 * cap, width), jnp.bfloat16),
            pltpu.VMEM((2, 3, cap, width), jnp.bfloat16),
            pltpu.VMEM((hidden, width), jnp.bfloat16),
            pltpu.VMEM((hidden, width), jnp.bfloat16),
            pltpu.VMEM((tok, 4 * cap), jnp.bfloat16),
            pltpu.VMEM((4, cap, width), jnp.bfloat16),
            pltpu.VMEM((4, cap, width), jnp.bfloat16),
            dma((2, 4, 4, 2)),
            dma((2, 4, 3)),
            dma((2, 4, 3)),
            dma((2, 4)),
            dma((2, 3)),
            dma((3,)),
            dma((3,)),
            dma((2,)),
        ],
        compiler_params=pltpu.CompilerParams(
            collective_id=0, has_side_effects=True, vmem_limit_bytes=58 * 1024 * 1024
        ),
        cost_estimate=pl.CostEstimate(
            flops=14 * 4 * cap * hidden * width, bytes_accessed=4 * hidden * width + 8 * f_own * width, transcendentals=8 * cap * hidden
        ),
    )(tokens, out_grad, gate.reshape(1, tok), region.reshape(1, tok), w_in[0], w_out[0])
    grad_scale = 1.0 / math.sqrt(float(tok * dp_count))
    return (token_grad, (grad_in * grad_scale)[None], (grad_out * grad_scale)[None])


def solution(mesh):
    small = mesh.shape["dp"] == 8 and mesh.shape["expert"] == 4
    return jax.shard_map(
        routed_local if small else local,
        mesh=mesh,
        in_specs=(
            P(("dp", "expert"), None),
            P(("dp", "expert"), None),
            P(("dp", "expert")),
            P(("dp", "expert"), None),
            P("expert", None, None),
            P("expert", None, None),
        ),
        out_specs=(P(("dp", "expert"), None), P("expert", "dp", None), P("expert", "dp", None)),
        check_vma=False,
    )
```

```python
import math

import jax
import jax.numpy as jnp
from jax import lax
from jax.experimental import pallas as pl
from jax.experimental.pallas import tpu as pltpu
from jax.sharding import PartitionSpec as P


MESH = pl.DeviceIdType.MESH
NT = (((1,), (1,)), ((), ()))
STEPS = [(0, 0, 1, 0), (0, 1, 0, 2), (1, 1, 1, 2), (0, 3, 1, 3), (2, 0, 3, 0), (2, 1, 2, 2), (3, 1, 3, 2)]


def gelu_halves(p):
    c = 0.7978845608028654
    square = p * p
    h = 0.5 + 0.5 * jnp.tanh(p * (c + (c * 0.044715) * square))
    value = p * h
    slope = h + value * (1.0 - h) * (2.0 * c + (6.0 * c * 0.044715) * square)
    return value, slope


def gelu_parts(pre_act):
    root_two_pi = 0.7978845608028654
    cubic = pre_act * pre_act * pre_act
    tanh_val = jnp.tanh(root_two_pi * (pre_act + 0.044715 * cubic))
    halved = 0.5 * (1.0 + tanh_val)
    gelu_value = pre_act * halved
    gelu_slope = halved + 0.5 * pre_act * (1.0 - tanh_val * tanh_val) * root_two_pi * (
        1.0 + 3.0 * 0.044715 * pre_act * pre_act
    )
    return (gelu_value, gelu_slope)


def expert_rows(inputs_win, grads_win, weight_in, weight_out):
    pre_act = lax.dot_general(
        inputs_win, weight_in, (((1,), (1,)), ((), ())), preferred_element_type=jnp.float32
    )
    gelu_value, gelu_slope = gelu_parts(pre_act)
    activation = gelu_value.astype(jnp.bfloat16)
    act_grad = lax.dot_general(
        grads_win, weight_out, (((1,), (1,)), ((), ())), preferred_element_type=jnp.float32
    )
    pre_grad = (act_grad * gelu_slope).astype(jnp.bfloat16)
    row_grads = jnp.dot(pre_grad, weight_in, preferred_element_type=jnp.float32).astype(
        jnp.bfloat16
    )
    return (activation, pre_grad, row_grads)


def send_back(row_grads):
    return lax.all_to_all(row_grads, "expert", split_axis=0, concat_axis=0, tiled=True)


def local(tokens, out_grad, gate, region, w_in, w_out):
    groups = lax.axis_size("expert")
    dp_count = lax.axis_size("dp")
    token_count = tokens.shape[0]
    model_width = tokens.shape[1]
    capacity = 2 * token_count // groups
    slot_count = groups * capacity
    region_ids = region[:, 0]
    onehot = (region_ids[:, None] == jnp.arange(groups, dtype=jnp.int32)[None, :]).astype(jnp.int32)
    rank_in = jnp.sum(jnp.cumsum(onehot, 0) * onehot, 1) - 1
    slot_ids = region_ids * capacity + rank_in
    scaled = (gate[:, None] * out_grad.astype(jnp.float32)).astype(jnp.bfloat16)
    send_x = jnp.zeros((slot_count, model_width), jnp.bfloat16).at[slot_ids].set(tokens)
    send_d = jnp.zeros((slot_count, model_width), jnp.bfloat16).at[slot_ids].set(scaled)
    recv_x, recv_d = (
        lax.all_to_all(send_x, "expert", split_axis=0, concat_axis=0, tiled=True),
        lax.all_to_all(send_d, "expert", split_axis=0, concat_axis=0, tiled=True),
    )
    weight_in = w_in[0]
    weight_out = w_out[0]
    activation, pre_grad, row_grads = expert_rows(recv_x, recv_d, weight_in, weight_out)
    grad_scale = 1.0 / math.sqrt(float(token_count * dp_count))
    returned = send_back(row_grads)
    summed = lax.psum_scatter(
        jnp.concatenate(
            [
                lax.dot_general(
                    pre_grad, recv_x, (((0,), (0,)), ((), ())), preferred_element_type=jnp.float32
                ),
                lax.dot_general(
                    activation, recv_d, (((0,), (0,)), ((), ())), preferred_element_type=jnp.float32
                ),
            ],
            axis=1,
        ).astype(jnp.bfloat16),
        "dp",
        scatter_dimension=0,
        tiled=True,
    ).astype(jnp.float32)
    grad_in = summed[:, :model_width]
    grad_out = summed[:, model_width:]
    token_grad = returned[slot_ids]
    return (token_grad, (grad_in * grad_scale)[None], (grad_out * grad_scale)[None])


def routed_kernel(
    tokens_ref, out_grad_ref, gate_ref, region_ref, w_in_hbm, w_out_hbm,
    token_grad_ref, grad_in_ref, grad_out_ref,
    sum_in, sum_out, rows, outbox, weight_in, weight_out, perm_back, row_grads, returned,
    recv_sem, own_sem, pair_sem, fwd_sem, z_sem, back_send_sem, back_recv_sem, weight_sem, result_sem,
):
    dp = lax.axis_index("dp")
    z = lax.axis_index("expert")
    core = dp % 2
    chip = dp // 2
    cx = chip % 2
    cy = chip // 2
    pair = dp + 1 - 2 * core
    along_x = (cy * 2 + 1 - cx) * 2 + core
    along_y = ((1 - cy) * 2 + cx) * 2 + core
    forward_to = along_y * (1 - core) + along_x * core
    peers = [z, z + 1 - 2 * (z % 2), (z + 2) % 4, 3 - z]
    tok = tokens_ref.shape[0]
    cap = rows.shape[3] // 2
    f_own = grad_in_ref.shape[0]

    def half(q, r, k, c):
        return rows.at[q, r, k, pl.ds(pl.multiple_of(c * cap, cap), cap)]

    def remote(src, dst, send, recv, where):
        return pltpu.make_async_remote_copy(
            src_ref=src, dst_ref=dst, send_sem=send, recv_sem=recv, device_id=where, device_id_type=MESH
        )

    def arrival(q, r, k, c):
        slot = half(q, r, k, c)
        return remote(slot, slot, own_sem.at[q, r, 0], recv_sem.at[q, r, k, c], (pair, z))

    def own_copies(q, r):
        src = half(q, r, 0, core)
        return [
            remote(src, half(q, r, 1, core), own_sem.at[q, r, 0], recv_sem.at[q, r, 1, core], (along_x, z)),
            remote(src, half(q, r, 2, core), own_sem.at[q, r, 1], recv_sem.at[q, r, 2, core], (along_y, z)),
            remote(src, half(q, r, 0, core), own_sem.at[q, r, 2], recv_sem.at[q, r, 0, core], (pair, z)),
        ]

    def forward_copy(q, r):
        return remote(
            half(q, r, 1 + core, core), half(q, r, 3, core), fwd_sem.at[q, r], recv_sem.at[q, r, 3, core], (forward_to, z)
        )

    def pair_copy(q, r, k):
        slot = half(q, r, k, core)
        return remote(slot, slot, pair_sem.at[q, r, k - 1], recv_sem.at[q, r, k, core], (pair, z))

    def z_copy(q, r):
        return remote(outbox.at[q, r - 1], half(q, r, 0, core), z_sem.at[q, r - 1], recv_sem.at[q, r, 0, core], (dp, peers[r]))

    def back_copy(r):
        return remote(
            row_grads.at[r], returned.at[r], back_send_sem.at[r - 1], back_recv_sem.at[r - 1], (dp, peers[r])
        )

    weight_copies = [
        pltpu.make_async_copy(w_in_hbm, weight_in, weight_sem.at[0]),
        pltpu.make_async_copy(w_out_hbm, weight_out, weight_sem.at[1]),
    ]
    for copy in weight_copies:
        copy.start()
    barrier = pltpu.get_barrier_semaphore()
    for where in [(pair, z), (along_x, z), (along_y, z)] + [(dp, peer) for peer in peers[1:]]:
        pl.semaphore_signal(barrier, inc=1, device_id=where, device_id_type=MESH)

    region = region_ref[...]
    onehot = (jnp.broadcast_to(region, (8, tok)) == lax.broadcasted_iota(jnp.int32, (8, tok), 0)).astype(jnp.float32)
    upto = lax.broadcasted_iota(jnp.int32, (tok, tok), 0) <= lax.broadcasted_iota(jnp.int32, (tok, tok), 1)
    counts = jnp.dot(
        onehot.astype(jnp.bfloat16), upto.astype(jnp.float32).astype(jnp.bfloat16), preferred_element_type=jnp.float32
    )
    rank = jnp.sum(onehot * counts, axis=0, keepdims=True) - 1.0
    slot_ids = region * cap + rank.astype(jnp.int32)
    places = lax.broadcasted_iota(jnp.int32, (cap, tok), 0)
    gates = jnp.broadcast_to(gate_ref[...], (cap, tok))

    def one_hot(r):
        return (places + peers[r] * cap) == slot_ids

    def route(r):
        here = one_hot(r)
        moved = here.astype(jnp.float32).astype(jnp.bfloat16)
        gate_rows = jnp.sum(jnp.where(here, gates, 0.0), axis=1, keepdims=True)
        inputs = jnp.dot(moved, tokens_ref[...], preferred_element_type=jnp.float32).astype(jnp.bfloat16)
        grads = jnp.dot(moved, out_grad_ref[...], preferred_element_type=jnp.float32)
        return inputs, (gate_rows * grads).astype(jnp.bfloat16)

    mine = pl.ds(pl.multiple_of(core * cap, cap), cap)
    pl.semaphore_wait(barrier, 6)
    for r in (2, 0, 1, 3):
        inputs, grads = route(r)
        if r == 0:
            rows[0, 0, 0, mine] = inputs
            rows[1, 0, 0, mine] = grads
            for q in (0, 1):
                for copy in own_copies(q, 0):
                    copy.start()
        else:
            outbox[0, r - 1] = inputs
            outbox[1, r - 1] = grads
            for q in (0, 1):
                z_copy(q, r).start()
    for r in range(4):
        perm_back[:, r * cap : (r + 1) * cap] = one_hot(r).astype(jnp.float32).T.astype(jnp.bfloat16)
    sum_in[...] = jnp.zeros_like(sum_in)
    sum_out[...] = jnp.zeros_like(sum_out)
    for copy in weight_copies:
        copy.wait()
    own_f = pl.ds(pl.multiple_of(dp * f_own, f_own), f_own)

    def weight_grads(places):
        for r, k in places:
            for q in (0, 1):
                arrival(q, r, k, 1 - core).wait_recv()
        inputs = jnp.concatenate([rows[0, r, k] for r, k in places], axis=0)
        grads = jnp.concatenate([rows[1, r, k] for r, k in places], axis=0)
        pre_act = lax.dot_general(weight_in[own_f], inputs, NT, preferred_element_type=jnp.float32)
        act_grad = lax.dot_general(weight_out[own_f], grads, NT, preferred_element_type=jnp.float32)
        value, slope = gelu_halves(pre_act)
        activation = value.astype(jnp.bfloat16)
        pre_grad = (act_grad * slope).astype(jnp.bfloat16)
        sum_in[...] += jnp.dot(pre_grad, inputs, preferred_element_type=jnp.float32)
        sum_out[...] += jnp.dot(activation, grads, preferred_element_type=jnp.float32)

    def input_grads(rounds):
        inputs = jnp.concatenate([rows[0, r, 0, mine] for r in rounds], axis=0)
        grads = jnp.concatenate([rows[1, r, 0, mine] for r in rounds], axis=0)

        def part(i, total):
            chunk = pl.ds(pl.multiple_of(i * 512, 512), 512)
            w = weight_in[chunk]
            pre_act = lax.dot_general(inputs, w, NT, preferred_element_type=jnp.float32)
            act_grad = lax.dot_general(grads, weight_out[chunk], NT, preferred_element_type=jnp.float32)
            pre_grad = (act_grad * gelu_halves(pre_act)[1]).astype(jnp.bfloat16)
            return total + jnp.dot(pre_grad, w, preferred_element_type=jnp.float32)

        zeros = jnp.zeros((len(rounds) * cap, tokens_ref.shape[1]), jnp.float32)
        total = lax.fori_loop(0, weight_in.shape[0] // 512, part, zeros).astype(jnp.bfloat16)
        for i, r in enumerate(rounds):
            row_grads[r] = total[i * cap : (i + 1) * cap]

    def from_z(r):
        for q in (0, 1):
            arrival(q, r, 0, core).wait_recv()
            for copy in own_copies(q, r):
                copy.start()

    def from_sides(r):
        for q in (0, 1):
            for k in (1, 2):
                arrival(q, r, k, core).wait_recv()
            forward_copy(q, r).start()
            for k in (1, 2):
                pair_copy(q, r, k).start()

    def from_diagonal(r):
        for q in (0, 1):
            arrival(q, r, 3, core).wait_recv()
            pair_copy(q, r, 3).start()

    def step(s, table):
        @pl.when((s == 0) | (s == 3) | (s == 4))
        def _():
            from_z(lax.max(s - 1, 1))

        @pl.when(s == 3)
        def _():
            input_grads((1, 2))
            back_copy(1).start()
            back_copy(2).start()
            from_diagonal(0)
            from_diagonal(1)

        @pl.when(s == 4)
        def _():
            input_grads((3,))
            back_copy(3).start()

        @pl.when((s == 1) | (s == 2) | (s == 5) | (s == 6))
        def _():
            from_sides(s - 1 - 2 * (s // 5))

        r1, k1, r2, k2 = [column % 4 for column in table]
        weight_grads([(r1, k1), (r2, k2)])
        return tuple(column // 4 for column in table)

    input_grads((0,))
    table = [0, 0, 0, 0]
    for s, entry in enumerate(STEPS):
        for i, digit in enumerate(entry):
            table[i] += digit * 4**s
    lax.fori_loop(0, len(STEPS), step, tuple(jnp.int32(column) for column in table))

    def last(r, carry):
        from_diagonal(r)
        weight_grads([(r, 3)])
        return carry

    lax.fori_loop(2, 4, last, 0)
    results = [
        pltpu.make_async_copy(sum_in, grad_in_ref, result_sem.at[0]),
        pltpu.make_async_copy(sum_out, grad_out_ref, result_sem.at[1]),
    ]
    for copy in results:
        copy.start()
    returned[0] = row_grads[0]
    for r in (1, 2, 3):
        back_copy(r).wait_recv()
    collected = returned[...].reshape(4 * cap, tokens_ref.shape[1])
    token_grad_ref[...] = jnp.dot(perm_back[...], collected, preferred_element_type=jnp.float32).astype(jnp.bfloat16)

    for r in (1, 2, 3):
        back_copy(r).wait_send()
        for q in (0, 1):
            z_copy(q, r).wait_send()

    def drain(r, carry):
        for q in (0, 1):
            for copy in own_copies(q, r):
                copy.wait_send()
            forward_copy(q, r).wait_send()
            for k in (1, 2, 3):
                pair_copy(q, r, k).wait_send()
        return carry

    lax.fori_loop(0, 4, drain, 0)
    for copy in results:
        copy.wait()


def routed_local(tokens, out_grad, gate, region, w_in, w_out):
    dp_count = lax.axis_size("dp")
    tok, width = tokens.shape
    cap = tok // 2
    hidden = w_in.shape[1]
    f_own = hidden // dp_count
    vmem = pl.BlockSpec(memory_space=pltpu.VMEM)
    hbm = pl.BlockSpec(memory_space=pl.ANY)
    dma = pltpu.SemaphoreType.DMA
    token_grad, grad_in, grad_out = pl.pallas_call(
        routed_kernel,
        out_shape=(
            jax.ShapeDtypeStruct((tok, width), jnp.bfloat16),
            jax.ShapeDtypeStruct((f_own, width), jnp.float32),
            jax.ShapeDtypeStruct((f_own, width), jnp.float32),
        ),
        in_specs=[vmem, vmem, vmem, vmem, hbm, hbm],
        out_specs=(vmem, hbm, hbm),
        scratch_shapes=[
            pltpu.VMEM((f_own, width), jnp.float32),
            pltpu.VMEM((f_own, width), jnp.float32),
            pltpu.VMEM((2, 4, 4, 2 * cap, width), jnp.bfloat16),
            pltpu.VMEM((2, 3, cap, width), jnp.bfloat16),
            pltpu.VMEM((hidden, width), jnp.bfloat16),
            pltpu.VMEM((hidden, width), jnp.bfloat16),
            pltpu.VMEM((tok, 4 * cap), jnp.bfloat16),
            pltpu.VMEM((4, cap, width), jnp.bfloat16),
            pltpu.VMEM((4, cap, width), jnp.bfloat16),
            dma((2, 4, 4, 2)),
            dma((2, 4, 3)),
            dma((2, 4, 3)),
            dma((2, 4)),
            dma((2, 3)),
            dma((3,)),
            dma((3,)),
            dma((2,)),
            dma((2,)),
        ],
        compiler_params=pltpu.CompilerParams(
            collective_id=0, has_side_effects=True, vmem_limit_bytes=54 * 1024 * 1024
        ),
        cost_estimate=pl.CostEstimate(
            flops=14 * 4 * cap * hidden * width, bytes_accessed=4 * hidden * width + 8 * f_own * width, transcendentals=8 * cap * hidden
        ),
    )(tokens, out_grad, gate.reshape(1, tok), region.reshape(1, tok), w_in[0], w_out[0])
    grad_scale = 1.0 / math.sqrt(float(tok * dp_count))
    return (token_grad, (grad_in * grad_scale)[None], (grad_out * grad_scale)[None])


def solution(mesh):
    small = mesh.shape["dp"] == 8 and mesh.shape["expert"] == 4
    return jax.shard_map(
        routed_local if small else local,
        mesh=mesh,
        in_specs=(
            P(("dp", "expert"), None),
            P(("dp", "expert"), None),
            P(("dp", "expert")),
            P(("dp", "expert"), None),
            P("expert", None, None),
            P("expert", None, None),
        ),
        out_specs=(P(("dp", "expert"), None), P("expert", "dp", None), P("expert", "dp", None)),
        check_vma=False,
    )
```

```python
import math

import jax
import jax.numpy as jnp
from jax import lax
from jax.experimental import pallas as pl
from jax.experimental.pallas import tpu as pltpu
from jax.sharding import PartitionSpec as P


MESH = pl.DeviceIdType.MESH
NT = (((1,), (1,)), ((), ()))
STEPS = [(0, 0, 1, 0), (0, 1, 0, 2), (1, 1, 1, 2), (0, 3, 1, 3), (2, 0, 3, 0), (2, 1, 2, 2), (3, 1, 3, 2)]


def gelu_halves(p):
    c = 0.7978845608028654
    square = p * p
    h = 0.5 + 0.5 * jnp.tanh(p * (c + (c * 0.044715) * square))
    value = p * h
    slope = h + value * (1.0 - h) * (2.0 * c + (6.0 * c * 0.044715) * square)
    return value, slope


def gelu_parts(pre_act):
    root_two_pi = 0.7978845608028654
    cubic = pre_act * pre_act * pre_act
    tanh_val = jnp.tanh(root_two_pi * (pre_act + 0.044715 * cubic))
    halved = 0.5 * (1.0 + tanh_val)
    gelu_value = pre_act * halved
    gelu_slope = halved + 0.5 * pre_act * (1.0 - tanh_val * tanh_val) * root_two_pi * (
        1.0 + 3.0 * 0.044715 * pre_act * pre_act
    )
    return (gelu_value, gelu_slope)


def expert_rows(inputs_win, grads_win, weight_in, weight_out):
    pre_act = lax.dot_general(
        inputs_win, weight_in, (((1,), (1,)), ((), ())), preferred_element_type=jnp.float32
    )
    gelu_value, gelu_slope = gelu_parts(pre_act)
    activation = gelu_value.astype(jnp.bfloat16)
    act_grad = lax.dot_general(
        grads_win, weight_out, (((1,), (1,)), ((), ())), preferred_element_type=jnp.float32
    )
    pre_grad = (act_grad * gelu_slope).astype(jnp.bfloat16)
    row_grads = jnp.dot(pre_grad, weight_in, preferred_element_type=jnp.float32).astype(
        jnp.bfloat16
    )
    return (activation, pre_grad, row_grads)


def send_back(row_grads):
    return lax.all_to_all(row_grads, "expert", split_axis=0, concat_axis=0, tiled=True)


def local(tokens, out_grad, gate, region, w_in, w_out):
    groups = lax.axis_size("expert")
    dp_count = lax.axis_size("dp")
    token_count = tokens.shape[0]
    model_width = tokens.shape[1]
    capacity = 2 * token_count // groups
    slot_count = groups * capacity
    region_ids = region[:, 0]
    onehot = (region_ids[:, None] == jnp.arange(groups, dtype=jnp.int32)[None, :]).astype(jnp.int32)
    rank_in = jnp.sum(jnp.cumsum(onehot, 0) * onehot, 1) - 1
    slot_ids = region_ids * capacity + rank_in
    scaled = (gate[:, None] * out_grad.astype(jnp.float32)).astype(jnp.bfloat16)
    send_x = jnp.zeros((slot_count, model_width), jnp.bfloat16).at[slot_ids].set(tokens)
    send_d = jnp.zeros((slot_count, model_width), jnp.bfloat16).at[slot_ids].set(scaled)
    recv_x, recv_d = (
        lax.all_to_all(send_x, "expert", split_axis=0, concat_axis=0, tiled=True),
        lax.all_to_all(send_d, "expert", split_axis=0, concat_axis=0, tiled=True),
    )
    weight_in = w_in[0]
    weight_out = w_out[0]
    activation, pre_grad, row_grads = expert_rows(recv_x, recv_d, weight_in, weight_out)
    grad_scale = 1.0 / math.sqrt(float(token_count * dp_count))
    returned = send_back(row_grads)
    summed = lax.psum_scatter(
        jnp.concatenate(
            [
                lax.dot_general(
                    pre_grad, recv_x, (((0,), (0,)), ((), ())), preferred_element_type=jnp.float32
                ),
                lax.dot_general(
                    activation, recv_d, (((0,), (0,)), ((), ())), preferred_element_type=jnp.float32
                ),
            ],
            axis=1,
        ).astype(jnp.bfloat16),
        "dp",
        scatter_dimension=0,
        tiled=True,
    ).astype(jnp.float32)
    grad_in = summed[:, :model_width]
    grad_out = summed[:, model_width:]
    token_grad = returned[slot_ids]
    return (token_grad, (grad_in * grad_scale)[None], (grad_out * grad_scale)[None])


def routed_kernel(
    tokens_ref, out_grad_ref, gate_ref, region_ref, w_in_hbm, w_out_hbm,
    token_grad_ref, grad_in_ref, grad_out_ref,
    sum_in, sum_out, rows, outbox, weight_in, weight_out, perm_back, row_grads, returned,
    recv_sem, own_sem, pair_sem, fwd_sem, z_sem, back_send_sem, back_recv_sem, weight_sem, result_sem,
):
    dp = lax.axis_index("dp")
    z = lax.axis_index("expert")
    core = dp % 2
    chip = dp // 2
    cx = chip % 2
    cy = chip // 2
    pair = dp + 1 - 2 * core
    along_x = (cy * 2 + 1 - cx) * 2 + core
    along_y = ((1 - cy) * 2 + cx) * 2 + core
    forward_to = along_y * (1 - core) + along_x * core
    peers = [z, z + 1 - 2 * (z % 2), (z + 2) % 4, 3 - z]
    tok = tokens_ref.shape[0]
    cap = rows.shape[3] // 2
    f_own = grad_in_ref.shape[0]

    def half(q, r, k, c):
        return rows.at[q, r, k, pl.ds(pl.multiple_of(c * cap, cap), cap)]

    def remote(src, dst, send, recv, where):
        return pltpu.make_async_remote_copy(
            src_ref=src, dst_ref=dst, send_sem=send, recv_sem=recv, device_id=where, device_id_type=MESH
        )

    def arrival(q, r, k, c):
        slot = half(q, r, k, c)
        return remote(slot, slot, own_sem.at[q, r, 0], recv_sem.at[q, r, k, c], (pair, z))

    def own_copies(q, r):
        src = half(q, r, 0, core)
        return [
            remote(src, half(q, r, 1, core), own_sem.at[q, r, 0], recv_sem.at[q, r, 1, core], (along_x, z)),
            remote(src, half(q, r, 2, core), own_sem.at[q, r, 1], recv_sem.at[q, r, 2, core], (along_y, z)),
            remote(src, half(q, r, 0, core), own_sem.at[q, r, 2], recv_sem.at[q, r, 0, core], (pair, z)),
        ]

    def forward_copy(q, r):
        return remote(
            half(q, r, 1 + core, core), half(q, r, 3, core), fwd_sem.at[q, r], recv_sem.at[q, r, 3, core], (forward_to, z)
        )

    def pair_copy(q, r, k):
        slot = half(q, r, k, core)
        return remote(slot, slot, pair_sem.at[q, r, k - 1], recv_sem.at[q, r, k, core], (pair, z))

    def z_copy(q, r, peer):
        return remote(outbox.at[q, r - 1], half(q, r, 0, core), z_sem.at[q, r - 1], recv_sem.at[q, r, 0, core], (dp, peer))

    def back_copy(r):
        return remote(
            row_grads.at[r], returned.at[r], back_send_sem.at[r - 1], back_recv_sem.at[r - 1], (dp, peers[r])
        )

    weight_copies = [
        pltpu.make_async_copy(w_in_hbm, weight_in, weight_sem.at[0]),
        pltpu.make_async_copy(w_out_hbm, weight_out, weight_sem.at[1]),
    ]
    for copy in weight_copies:
        copy.start()
    barrier = pltpu.get_barrier_semaphore()
    for where in [(pair, z), (along_x, z), (along_y, z)] + [(dp, peer) for peer in peers[1:]]:
        pl.semaphore_signal(barrier, inc=1, device_id=where, device_id_type=MESH)

    region = region_ref[...]
    onehot = (jnp.broadcast_to(region, (8, tok)) == lax.broadcasted_iota(jnp.int32, (8, tok), 0)).astype(jnp.float32)
    upto = lax.broadcasted_iota(jnp.int32, (tok, tok), 0) <= lax.broadcasted_iota(jnp.int32, (tok, tok), 1)
    counts = jnp.dot(
        onehot.astype(jnp.bfloat16), upto.astype(jnp.float32).astype(jnp.bfloat16), preferred_element_type=jnp.float32
    )
    rank = jnp.sum(onehot * counts, axis=0, keepdims=True) - 1.0
    slot_ids = region * cap + rank.astype(jnp.int32)
    places = lax.broadcasted_iota(jnp.int32, (cap, tok), 0)
    gates = jnp.broadcast_to(gate_ref[...], (cap, tok))

    def one_hot(peer):
        return (places + peer * cap) == slot_ids

    def route(peer):
        here = one_hot(peer)
        moved = here.astype(jnp.float32).astype(jnp.bfloat16)
        gate_rows = jnp.sum(jnp.where(here, gates, 0.0), axis=1, keepdims=True)
        inputs = jnp.dot(moved, tokens_ref[...], preferred_element_type=jnp.float32).astype(jnp.bfloat16)
        grads = jnp.dot(moved, out_grad_ref[...], preferred_element_type=jnp.float32)
        return inputs, (gate_rows * grads).astype(jnp.bfloat16)

    mine = pl.ds(pl.multiple_of(core * cap, cap), cap)
    pl.semaphore_wait(barrier, 6)
    middle = ((z + 1) // 2) % 2
    near = peers[1] * (1 - middle) + peers[2] * middle
    far = peers[1] * middle + peers[2] * (1 - middle)
    for i, (r, peer) in enumerate(((1 + middle, near), (0, z), (2 - middle, far), (3, peers[3]))):
        inputs, grads = route(peer)
        if i == 1:
            rows[0, 0, 0, mine] = inputs
            rows[1, 0, 0, mine] = grads
            for q in (0, 1):
                for copy in own_copies(q, 0):
                    copy.start()
        else:
            outbox[0, r - 1] = inputs
            outbox[1, r - 1] = grads
            for q in (0, 1):
                z_copy(q, r, peer).start()
    for r in range(4):
        perm_back[:, r * cap : (r + 1) * cap] = one_hot(peers[r]).astype(jnp.float32).T.astype(jnp.bfloat16)
    sum_in[...] = jnp.zeros_like(sum_in)
    sum_out[...] = jnp.zeros_like(sum_out)
    for copy in weight_copies:
        copy.wait()
    own_f = pl.ds(pl.multiple_of(dp * f_own, f_own), f_own)

    def weight_grads(places):
        for r, k in places:
            for q in (0, 1):
                arrival(q, r, k, 1 - core).wait_recv()
        inputs = jnp.concatenate([rows[0, r, k] for r, k in places], axis=0)
        grads = jnp.concatenate([rows[1, r, k] for r, k in places], axis=0)
        pre_act = lax.dot_general(weight_in[own_f], inputs, NT, preferred_element_type=jnp.float32)
        act_grad = lax.dot_general(weight_out[own_f], grads, NT, preferred_element_type=jnp.float32)
        value, slope = gelu_halves(pre_act)
        activation = value.astype(jnp.bfloat16)
        pre_grad = (act_grad * slope).astype(jnp.bfloat16)
        sum_in[...] += jnp.dot(pre_grad, inputs, preferred_element_type=jnp.float32)
        sum_out[...] += jnp.dot(activation, grads, preferred_element_type=jnp.float32)

    def input_grads(rounds):
        inputs = jnp.concatenate([rows[0, r, 0, mine] for r in rounds], axis=0)
        grads = jnp.concatenate([rows[1, r, 0, mine] for r in rounds], axis=0)

        def part(i, total):
            chunk = pl.ds(pl.multiple_of(i * 512, 512), 512)
            w = weight_in[chunk]
            pre_act = lax.dot_general(inputs, w, NT, preferred_element_type=jnp.float32)
            act_grad = lax.dot_general(grads, weight_out[chunk], NT, preferred_element_type=jnp.float32)
            pre_grad = (act_grad * gelu_halves(pre_act)[1]).astype(jnp.bfloat16)
            return total + jnp.dot(pre_grad, w, preferred_element_type=jnp.float32)

        zeros = jnp.zeros((len(rounds) * cap, tokens_ref.shape[1]), jnp.float32)
        total = lax.fori_loop(0, weight_in.shape[0] // 512, part, zeros).astype(jnp.bfloat16)
        for i, r in enumerate(rounds):
            row_grads[r] = total[i * cap : (i + 1) * cap]

    def from_z(r):
        for q in (0, 1):
            arrival(q, r, 0, core).wait_recv()
            for copy in own_copies(q, r):
                copy.start()

    def from_sides(r):
        for q in (0, 1):
            for k in (1, 2):
                arrival(q, r, k, core).wait_recv()
            forward_copy(q, r).start()
            for k in (1, 2):
                pair_copy(q, r, k).start()

    def from_diagonal(r):
        for q in (0, 1):
            arrival(q, r, 3, core).wait_recv()
            pair_copy(q, r, 3).start()

    def step(s, table):
        @pl.when((s == 0) | (s == 3) | (s == 4))
        def _():
            from_z(lax.max(s - 1, 1))

        @pl.when(s == 3)
        def _():
            input_grads((1, 2))
            back_copy(1).start()
            back_copy(2).start()
            from_diagonal(0)
            from_diagonal(1)

        @pl.when(s == 4)
        def _():
            input_grads((3,))
            back_copy(3).start()

        @pl.when((s == 1) | (s == 2) | (s == 5) | (s == 6))
        def _():
            from_sides(s - 1 - 2 * (s // 5))

        r1, k1, r2, k2 = [column % 4 for column in table]
        weight_grads([(r1, k1), (r2, k2)])
        return tuple(column // 4 for column in table)

    input_grads((0,))
    table = [0, 0, 0, 0]
    for s, entry in enumerate(STEPS):
        for i, digit in enumerate(entry):
            table[i] += digit * 4**s
    lax.fori_loop(0, len(STEPS), step, tuple(jnp.int32(column) for column in table))

    def last(r, carry):
        from_diagonal(r)
        weight_grads([(r, 3)])
        return carry

    lax.fori_loop(2, 4, last, 0)
    results = [
        pltpu.make_async_copy(sum_in, grad_in_ref, result_sem.at[0]),
        pltpu.make_async_copy(sum_out, grad_out_ref, result_sem.at[1]),
    ]
    for copy in results:
        copy.start()
    returned[0] = row_grads[0]
    for r in (1, 2, 3):
        back_copy(r).wait_recv()
    collected = returned[...].reshape(4 * cap, tokens_ref.shape[1])
    token_grad_ref[...] = jnp.dot(perm_back[...], collected, preferred_element_type=jnp.float32).astype(jnp.bfloat16)

    for r in (1, 2, 3):
        back_copy(r).wait_send()
        for q in (0, 1):
            z_copy(q, r, peers[r]).wait_send()

    def drain(r, carry):
        for q in (0, 1):
            for copy in own_copies(q, r):
                copy.wait_send()
            forward_copy(q, r).wait_send()
            for k in (1, 2, 3):
                pair_copy(q, r, k).wait_send()
        return carry

    lax.fori_loop(0, 4, drain, 0)
    for copy in results:
        copy.wait()


def routed_local(tokens, out_grad, gate, region, w_in, w_out):
    dp_count = lax.axis_size("dp")
    tok, width = tokens.shape
    cap = tok // 2
    hidden = w_in.shape[1]
    f_own = hidden // dp_count
    vmem = pl.BlockSpec(memory_space=pltpu.VMEM)
    hbm = pl.BlockSpec(memory_space=pl.ANY)
    dma = pltpu.SemaphoreType.DMA
    token_grad, grad_in, grad_out = pl.pallas_call(
        routed_kernel,
        out_shape=(
            jax.ShapeDtypeStruct((tok, width), jnp.bfloat16),
            jax.ShapeDtypeStruct((f_own, width), jnp.float32),
            jax.ShapeDtypeStruct((f_own, width), jnp.float32),
        ),
        in_specs=[vmem, vmem, vmem, vmem, hbm, hbm],
        out_specs=(vmem, hbm, hbm),
        scratch_shapes=[
            pltpu.VMEM((f_own, width), jnp.float32),
            pltpu.VMEM((f_own, width), jnp.float32),
            pltpu.VMEM((2, 4, 4, 2 * cap, width), jnp.bfloat16),
            pltpu.VMEM((2, 3, cap, width), jnp.bfloat16),
            pltpu.VMEM((hidden, width), jnp.bfloat16),
            pltpu.VMEM((hidden, width), jnp.bfloat16),
            pltpu.VMEM((tok, 4 * cap), jnp.bfloat16),
            pltpu.VMEM((4, cap, width), jnp.bfloat16),
            pltpu.VMEM((4, cap, width), jnp.bfloat16),
            dma((2, 4, 4, 2)),
            dma((2, 4, 3)),
            dma((2, 4, 3)),
            dma((2, 4)),
            dma((2, 3)),
            dma((3,)),
            dma((3,)),
            dma((2,)),
            dma((2,)),
        ],
        compiler_params=pltpu.CompilerParams(
            collective_id=0, has_side_effects=True, vmem_limit_bytes=54 * 1024 * 1024
        ),
        cost_estimate=pl.CostEstimate(
            flops=14 * 4 * cap * hidden * width, bytes_accessed=4 * hidden * width + 8 * f_own * width, transcendentals=8 * cap * hidden
        ),
    )(tokens, out_grad, gate.reshape(1, tok), region.reshape(1, tok), w_in[0], w_out[0])
    grad_scale = 1.0 / math.sqrt(float(tok * dp_count))
    return (token_grad, (grad_in * grad_scale)[None], (grad_out * grad_scale)[None])


def solution(mesh):
    small = mesh.shape["dp"] == 8 and mesh.shape["expert"] == 4
    return jax.shard_map(
        routed_local if small else local,
        mesh=mesh,
        in_specs=(
            P(("dp", "expert"), None),
            P(("dp", "expert"), None),
            P(("dp", "expert")),
            P(("dp", "expert"), None),
            P("expert", None, None),
            P("expert", None, None),
        ),
        out_specs=(P(("dp", "expert"), None), P("expert", "dp", None), P("expert", "dp", None)),
        check_vma=False,
    )
```
